512 devices in a mesh: dp: 2 (over core), ctx: 64 (over z, y), tp: 4 (over x).
Axes of the slice: x: 4, y: 4, z: 16, core: 2. Of those that a mesh axis runs over, the one named last changes fastest.
Arguments:
- query_proj: bfloat16 [2, 8192, 8192], P('dp', 'tp', 'ctx'), may hold values from -6 to 6
- key_proj: bfloat16 [2, 8192, 8192], P('dp', 'tp', 'ctx'), may hold values from -6 to 6
- value_proj: bfloat16 [2, 8192, 8192], P('dp', 'tp', 'ctx'), may hold values from -6 to 6
- out_grad: bfloat16 [2, 8192, 8192], P('dp', ('ctx', 'tp')), may hold values from -6 to 6
- filter_taps: bfloat16 [4, 2048, 8192], P('tp', 'ctx'), may hold values from -1 to 1
- skip_gain: float32 [4, 2048], P('tp'), may hold values from -3 to 3
Outputs:
- query_grad: bfloat16 [2, 8192, 8192], P('dp', 'tp', 'ctx')
- key_grad: bfloat16 [2, 8192, 8192], P('dp', 'tp', 'ctx')
- value_grad: bfloat16 [2, 8192, 8192], P('dp', 'tp', 'ctx')
- filter_grad: float32 [4, 2048, 8192], P('tp', 'ctx', 'dp')
The draws below stay inside these ranges and needn't reach their ends.
All inputs are finite; a program needn't handle non-finite values.
Results may differ from the reference program's by a relative error of at most 0.01.
Values may be sent and summed in bfloat16 or wider, within the bound.
No kernel may reach another device: no remote copies, remote signals or barrier semaphores. Data moves between devices by JAX's collectives and lax.ppermute only.
A program may use at most 64 MiB of HBM per device.

```python
import math
import jax
import jax.numpy as jnp
from jax import lax

D = 8192
L_DEV = 128
L = 8192
SEQS = 2
BLOCKS = 128
NFFT = 16384
GROUPS = 4
GROUP_CH = 2048


def draw_filter_taps(key, part):
    key = jax.random.fold_in(key, 7)
    key_scale, key_noise = jax.random.split(key, 2)
    tap_count = L
    log_scale = jax.random.uniform(key_scale, (D,), jnp.float32, math.log(30.0), math.log(8.0 * tap_count))
    noise_field = jax.random.truncated_normal(key_noise, -4.0, 4.0, (D, tap_count), jnp.float32)
    time_scale = jnp.exp(log_scale)
    amplitude = jnp.sqrt(2.0 / jnp.minimum(time_scale, tap_count * 1.0))
    position = jnp.arange(tap_count).astype(jnp.float32)
    values_out = amplitude[:, None] * noise_field * jnp.exp(-position[None, :] / time_scale[:, None])
    values_out = jnp.clip(values_out, -1.0, 1.0)
    return values_out.reshape(GROUPS, GROUP_CH, tap_count).astype(jnp.bfloat16)


def steps_of(rng, dims, cuts, smallest, largest):
    def one(dim, parts):
        draws = jax.random.uniform(jax.random.fold_in(jax.random.fold_in(rng, 6), dim), (parts,), jnp.float32, smallest / len(cuts), largest / len(cuts))
        return jnp.repeat(jnp.exp(draws), dims[dim] // parts).reshape((-1,) + (1,) * (len(dims) - dim - 1))

    gain = one(*cuts[0])
    for cut in cuts[1:]:
        gain = gain * one(*cut)
    return gain


def noise(rng, dims, spread, reach, shards=(), dtype=jnp.bfloat16):
    level = steps_of(rng, dims, shards, -0.22, 0.18) if shards else 1.0
    values = jax.random.normal(rng, dims, jnp.float32) * spread * level
    return jnp.minimum(jnp.maximum(values, -reach), reach).astype(dtype)


def setup_inputs(seed: int = 0) -> dict:
    seeds = jax.random.split(jax.random.key(seed), 7)
    return {
        "query_proj": noise(seeds[0], (SEQS, D, L), 1.0, 6.0, ((0, 2), (1, 4), (2, 64))),
        "key_proj": noise(seeds[1], (SEQS, D, L), 1.0, 6.0, ((0, 2), (1, 4), (2, 64))),
        "value_proj": noise(seeds[2], (SEQS, D, L), 1.0, 6.0, ((0, 2), (1, 4), (2, 64))),
        "out_grad": noise(seeds[3], (SEQS, L, D), 1.0, 6.0, ((0, 2), (1, 256))),
        "filter_taps": draw_filter_taps(jax.random.fold_in(seeds[6], 71), 0),
        "skip_gain": noise(seeds[5], (GROUPS, GROUP_CH), 0.5, 3.0, ((0, 4),), jnp.float32),
    }


def angle_table(row_count, col_count, modulus):
    row_index = lax.broadcasted_iota(jnp.int32, (row_count, col_count), 0)
    col_index = lax.broadcasted_iota(jnp.int32, (row_count, col_count), 1)
    product = row_index * col_index % modulus
    return product.astype(jnp.float32) * (2.0 * math.pi / modulus)

def make_tables(block_rows, local_len):
    half_rows = block_rows // 2
    angle_fwd = angle_table(block_rows, half_rows, block_rows)
    fwd_rows = jnp.concatenate([jnp.cos(angle_fwd), -jnp.sin(angle_fwd)], axis=0).astype(jnp.bfloat16)
    angle_twid = angle_table(block_rows, local_len, block_rows * local_len)
    twid_cos = jnp.cos(angle_twid)
    twid_sin = -jnp.sin(angle_twid)
    angle_small = angle_table(local_len, local_len, local_len)
    cos_small = jnp.cos(angle_small)
    sin_small = -jnp.sin(angle_small)
    mat_fwd = jnp.concatenate([jnp.concatenate([cos_small, sin_small], axis=1), jnp.concatenate([-sin_small, cos_small], axis=1)], axis=0).astype(jnp.bfloat16)
    mat_inv = jnp.concatenate([jnp.concatenate([cos_small, -sin_small], axis=1), jnp.concatenate([sin_small, cos_small], axis=1)], axis=0).astype(jnp.bfloat16)
    angle_back = angle_table(half_rows, block_rows, block_rows)
    back_rows = jnp.concatenate([jnp.cos(angle_back), -jnp.sin(angle_back)], axis=1).astype(jnp.bfloat16)
    return (fwd_rows, twid_cos, twid_sin, mat_fwd, mat_inv, back_rows)

def finish_forward(section_rows, twid_cos, twid_sin, mat_fwd):
    row_split = section_rows.shape[0] // 2
    real_rows = section_rows[:row_split]
    imag_rows = section_rows[row_split:]
    tcos = twid_cos[:, None, :]
    tsin = twid_sin[:, None, :]
    mixed = jnp.concatenate([real_rows * tcos - imag_rows * tsin, real_rows * tsin + imag_rows * tcos], axis=-1).astype(jnp.bfloat16)
    result = jnp.einsum('kcj,jq->kcq', mixed.astype(jnp.float32), mat_fwd.astype(jnp.float32), precision=lax.Precision.HIGHEST)
    col_split = result.shape[-1] // 2
    return (result[..., :col_split], result[..., col_split:])

def forward_transform(signal, tables):
    fwd_rows, twid_cos, twid_sin, mat_fwd, mat_inv, back_rows = tables
    channel_count = signal.shape[0]
    half_rows = fwd_rows.shape[1]
    local_len = mat_fwd.shape[0] // 2
    shaped = signal.reshape(channel_count, half_rows, local_len)
    section_rows = jnp.einsum('kn,cnq->kcq', fwd_rows.astype(jnp.float32), shaped.astype(jnp.float32), precision=lax.Precision.HIGHEST)
    return finish_forward(section_rows, twid_cos, twid_sin, mat_fwd)

def inverse_transform(spec_real, spec_imag, tables, factor):
    fwd_rows, twid_cos, twid_sin, mat_fwd, mat_inv, back_rows = tables
    joined = jnp.concatenate([spec_real, spec_imag], axis=-1).astype(jnp.bfloat16)
    mixed = jnp.einsum('kcj,jq->kcq', joined.astype(jnp.float32), mat_inv.astype(jnp.float32), precision=lax.Precision.HIGHEST)
    col_split = mixed.shape[-1] // 2
    real_part = mixed[..., :col_split]
    imag_part = mixed[..., col_split:]
    tcos = twid_cos[:, None, :]
    tsin = twid_sin[:, None, :]
    stacked = jnp.concatenate([real_part * tcos + imag_part * tsin, imag_part * tcos - real_part * tsin], axis=0).astype(jnp.bfloat16)
    result = jnp.einsum('mk,kcq->cmq', back_rows.astype(jnp.float32), stacked.astype(jnp.float32), precision=lax.Precision.HIGHEST)
    return (result * factor).reshape(result.shape[0], -1)

def reference(query_proj, key_proj, value_proj, out_grad, filter_taps, skip_gain):
    tables = make_tables(BLOCKS, L_DEV)
    block_size = math.gcd(D, 256)
    block_count = D // block_size
    factor = 1.0 / NFFT
    grad_tokens = jnp.transpose(out_grad, (0, 2, 1))

    def split_blocks(array):
        return array.reshape(SEQS, block_count, block_size, L).transpose(1, 0, 2, 3)
    taps_blocks = filter_taps.reshape(block_count, block_size, L)
    gain_blocks = skip_gain.reshape(block_count, block_size)

    def one_block(block_items):
        queries, keys_in, values_in, grads_in, taps_in, gains_in = block_items
        filt_re, filt_im = forward_transform(taps_in, tables)
        gains_col = gains_in[:, None]
        query_list = []
        key_list = []
        value_list = []
        lag_total = jnp.zeros((block_size, L), jnp.float32)
        for seq_index in range(SEQS):
            query_seq = queries[seq_index].astype(jnp.float32)
            key_seq = keys_in[seq_index].astype(jnp.float32)
            value_seq = values_in[seq_index].astype(jnp.float32)
            grad_seq = grads_in[seq_index].astype(jnp.float32)
            gated_in = (key_seq * value_seq).astype(jnp.bfloat16)
            gate_grad = (grad_seq * query_seq).astype(jnp.bfloat16)
            gated_re, gated_im = forward_transform(gated_in, tables)
            grad_re, grad_im = forward_transform(gate_grad, tables)
            conv_out = inverse_transform(filt_re * gated_re - filt_im * gated_im, filt_re * gated_im + filt_im * gated_re, tables, factor).astype(jnp.bfloat16)
            corr_out = inverse_transform(filt_re * grad_re + filt_im * grad_im, filt_re * grad_im - filt_im * grad_re, tables, factor).astype(jnp.bfloat16)
            lag_part = inverse_transform(gated_re * grad_re + gated_im * grad_im, gated_re * grad_im - gated_im * grad_re, tables, factor)
            lag_total = lag_total + lag_part
            query_list.append((grad_seq * (conv_out.astype(jnp.float32) + gains_col * gated_in.astype(jnp.float32))).astype(jnp.bfloat16))
            gated_total = corr_out.astype(jnp.float32) + gains_col * gate_grad.astype(jnp.float32)
            key_list.append((gated_total * value_seq).astype(jnp.bfloat16))
            value_list.append((gated_total * key_seq).astype(jnp.bfloat16))
        return (jnp.stack(query_list), jnp.stack(key_list), jnp.stack(value_list), lag_total)
    query_b, key_b, value_b, lag_b = lax.map(one_block, (split_blocks(query_proj), split_blocks(key_proj), split_blocks(value_proj), split_blocks(grad_tokens), taps_blocks, gain_blocks))

    def join_blocks(array):
        return array.transpose(1, 0, 2, 3).reshape(SEQS, D, L)
    grad_scale = 1.0 / math.sqrt(SEQS * L)
    filter_grad = (lag_b * grad_scale).reshape(GROUPS, GROUP_CH, L)
    return (join_blocks(query_b), join_blocks(key_b), join_blocks(value_b), filter_grad)
```

```python
import functools
import math

import jax
import jax.numpy as jnp
import numpy as np
from jax import lax
from jax.experimental import pallas as pl
from jax.experimental.pallas import tpu as pltpu
from jax.sharding import PartitionSpec as P

BF = jnp.bfloat16
F32 = jnp.float32


def angle(rows, cols, modulus):
    product = np.arange(rows)[:, None] * np.arange(cols)[None, :] % modulus
    return product.astype(np.float32) * np.float32(2.0 * math.pi / modulus)


def make_tables(block_rows, local_len, factor):
    half = block_rows // 2
    kept = half + 1
    rows = -(-kept // 16) * 16
    real = (np.arange(rows) < kept).astype(np.float32)[:, None]
    weight = np.where((np.arange(rows) == 0) | (np.arange(rows) == half), 1.0, 2.0)[:, None] * real
    fwd = angle(rows, half, block_rows)
    fwd_rows = np.concatenate([np.cos(fwd) * real, -np.sin(fwd) * real], axis=0)
    back_rows = np.concatenate([np.cos(fwd) * weight, -np.sin(fwd) * weight], axis=0).T * factor
    twid = angle(rows, local_len, block_rows * local_len)
    small = angle(local_len, local_len, local_len)
    c, s = np.cos(small), -np.sin(small)
    mat_fwd = np.block([[c, s], [-s, c]])
    mat_inv = np.block([[c, -s], [s, c]])
    pair = lambda a: np.concatenate([a, a], axis=1)
    return (
        jnp.asarray(fwd_rows, BF),
        jnp.asarray(back_rows, BF),
        jnp.asarray(pair(np.cos(twid)), F32),
        jnp.asarray(pair(-np.sin(twid)), F32),
        jnp.asarray(mat_fwd, BF),
        jnp.asarray(mat_inv, BF),
    )


def dot(a, b):
    return jnp.dot(a, b, preferred_element_type=F32)


def forward(blocks, fwd, tcos, tsin, mat, mixed):
    rows = fwd.shape[0] // 2
    n = blocks[0].shape[-1]
    tc, ts = tcos[...], tsin[...]
    for c in range(0, len(blocks), 2):
        a = dot(fwd[...], jnp.concatenate(blocks[c : c + 2], axis=-1))
        ar, ai = a[:rows], a[rows:]
        re = (ar * tc - ai * ts).astype(BF)
        im = (ar * ts + ai * tc).astype(BF)
        for j in range(2):
            at = pl.ds((c + j) * rows, rows)
            mixed[at, :n] = re[:, j * n : (j + 1) * n]
            mixed[at, n:] = im[:, j * n : (j + 1) * n]
    return dot(mixed[...], mat[...])


def inverse(re, im, back, tcos, tsin, mat):
    rows = back.shape[1] // 2
    n = re.shape[-1]
    tc, ts = tcos[...], tsin[...]
    e = dot(jnp.concatenate([re, im], axis=-1).astype(BF), mat[...])
    out = []
    for c in range(0, e.shape[0], 2 * rows):
        e0, e1 = e[c : c + rows], e[c + rows : c + 2 * rows]
        er = jnp.concatenate([e0[:, :n], e1[:, :n]], axis=-1)
        ei = jnp.concatenate([e0[:, n:], e1[:, n:]], axis=-1)
        g = jnp.concatenate([er * tc + ei * ts, ei * tc - er * ts], axis=0).astype(BF)
        o = dot(back[...], g)
        out += [o[:, :n], o[:, n:]]
    return out


def split(spec):
    n = spec.shape[-1] // 2
    return spec[:, :n], spec[:, n:]


def by_channel(ref):
    a = jnp.swapaxes(ref[...].astype(F32), 0, 1).astype(BF)
    return [a[c] for c in range(a.shape[0])]


def by_block(parts):
    return jnp.swapaxes(jnp.stack(parts), 0, 1).astype(BF)


def conv_kernel(x, taps, fwd, back, tc, ts, mf, mi, conv, f_spec, x_spec, mixed):
    f = forward([taps[c] for c in range(taps.shape[0])], fwd, tc, ts, mf, mixed)
    f_spec[...] = f
    s = forward(by_channel(x), fwd, tc, ts, mf, mixed)
    x_spec[...] = s
    fr, fi = split(f)
    xr, xi = split(s)
    conv[...] = by_block(inverse(fr * xr - fi * xi, fr * xi + fi * xr, back, tc, ts, mi))


def corr_kernel(x, conv, f_spec, fwd, back, tc, ts, mf, mi, both, g_spec, mixed):
    s = forward(by_channel(x), fwd, tc, ts, mf, mixed)
    g_spec[...] = s
    fr, fi = split(f_spec[...])
    gr, gi = split(s)
    both[:, 0] = conv[...]
    both[:, 1] = by_block(inverse(fr * gr + fi * gi, fr * gi - fi * gr, back, tc, ts, mi))


def lag_kernel(x_spec, g_spec, own_rows, away_rows, tc, ts, mi, own, away):
    xr, xi = split(x_spec[...])
    gr, gi = split(g_spec[...])
    rows = own_rows.shape[0]
    both = jnp.concatenate([own_rows[...], away_rows[...]], axis=0)
    parts = inverse(xr * gr + xi * gi, xr * gi - xi * gr, both, tc, ts, mi)
    for c, part in enumerate(parts):
        own[c] = part[:rows]
        away[c] = part[rows:].astype(BF)


def call(body, grid, ins, tables, outs, mixed=None):
    def cut(a, dim):
        block = tuple(s // grid if i == dim else s for i, s in enumerate(a.shape))
        return pl.BlockSpec(block, lambda g: tuple(g if i == dim else 0 for i in range(len(block))))

    def whole(a):
        return pl.BlockSpec(a.shape, lambda g: (0,) * len(a.shape))

    return pl.pallas_call(
        body,
        grid=(grid,),
        in_specs=[cut(a, d) for a, d in ins] + [whole(a) for a in tables],
        out_specs=[cut(a, d) for a, d in outs],
        out_shape=[a for a, _ in outs],
        scratch_shapes=[] if mixed is None else [pltpu.VMEM(mixed, BF)],
        compiler_params=pltpu.CompilerParams(vmem_limit_bytes=40 * 2**20),
        cost_estimate=pl.CostEstimate(flops=2**20, bytes_accessed=2**20, transcendentals=0),
    )(*[a for a, _ in ins], *tables)


def local(query_proj, key_proj, value_proj, out_grad, filter_taps, skip_gain):
    ctx = lax.axis_size("ctx")
    tp = lax.axis_size("tp")
    dp = lax.axis_size("dp")
    q, k, v = query_proj[0], key_proj[0], value_proj[0]
    chans, block = q.shape
    own = chans // ctx
    factor = 1.0 / (2 * ctx * block)
    fwd, back, tc, ts, mf, mi = make_tables(2 * ctx, block, factor)
    x = lax.axis_index("tp")
    core = lax.axis_index("dp")
    grid = 2
    spec = jax.ShapeDtypeStruct((own * tc.shape[0], 2 * block), F32)
    mixed = (spec.shape[0] // grid, 2 * block)

    def exchange(a):
        return lax.all_to_all(a, "ctx", split_axis=0, concat_axis=0, tiled=True)

    gated_in = (k.astype(F32) * v.astype(F32)).astype(BF)
    gated_c = exchange(gated_in.reshape(ctx, own, block))

    rows = out_grad[0]
    rows_per = rows.shape[0]
    parts = []
    for d in range(tp):
        piece = lax.dynamic_slice_in_dim(rows, lax.rem(x + d, tp) * chans, chans, axis=1)
        if d:
            piece = lax.ppermute(piece, "tp", [(j, (j + d) % tp) for j in range(tp)])
        parts.append(piece)
    order = [parts[(tp - 1 - i) % tp] for i in range(2 * tp - 1)]
    ring = jnp.concatenate(order, axis=0)
    grad_rows = lax.dynamic_slice_in_dim(ring, (tp - 1 - x) * rows_per, tp * rows_per, axis=0)
    grad_tokens = jnp.transpose(grad_rows)
    gate_grad = (grad_tokens.astype(F32) * q.astype(F32)).astype(BF)
    gated_c, gate_grad_c = lax.optimization_barrier((gated_c, gate_grad))
    grad_c = exchange(gate_grad_c.reshape(ctx, own, block))

    taps = filter_taps[0].reshape(own, ctx, block)
    tables = (fwd, back, tc, ts, mf, mi)
    block_out = jax.ShapeDtypeStruct((ctx, own, block), BF)
    conv, f_spec, x_spec = call(
        conv_kernel, grid, [(gated_c, 1), (taps, 0)], tables,
        [(block_out, 1), (spec, 0), (spec, 0)], mixed,
    )
    both, g_spec = call(
        corr_kernel, grid, [(grad_c, 1), (conv, 1), (f_spec, 0)], tables,
        [(jax.ShapeDtypeStruct((ctx, 2, own, block), BF), 2), (spec, 0)], mixed,
    )
    both = exchange(both.reshape(ctx, 2 * own, block)).reshape(ctx, 2, own, block)

    halves = back.reshape(dp, ctx // dp, -1)
    half_out = (own, ctx // dp, block)
    lag_own, lag_away = call(
        lag_kernel, grid, [(x_spec, 0), (g_spec, 0)],
        (
            lax.dynamic_index_in_dim(halves, core, keepdims=False),
            lax.dynamic_index_in_dim(halves, lax.rem(core + 1, dp), keepdims=False),
            tc, ts, mi,
        ),
        [(jax.ShapeDtypeStruct(half_out, F32), 0), (jax.ShapeDtypeStruct(half_out, BF), 0)],
    )
    other = lax.ppermute(lag_away, "dp", [(j, (j + 1) % dp) for j in range(dp)])
    grad_scale = 1.0 / math.sqrt(dp * ctx * block)
    filter_out = ((lag_own + other.astype(F32)) * grad_scale).reshape(1, own, -1)

    skip = skip_gain[0][:, None]
    conv_rows = both[:, 0].reshape(chans, block).astype(F32)
    corr_rows = both[:, 1].reshape(chans, block).astype(F32)
    query_out = (grad_tokens.astype(F32) * (conv_rows + skip * gated_in.astype(F32))).astype(BF)
    total = corr_rows + skip * gate_grad.astype(F32)
    key_out = (total * v.astype(F32)).astype(BF)
    value_out = (total * k.astype(F32)).astype(BF)
    return (query_out[None], key_out[None], value_out[None], filter_out)


def solution(mesh):
    assert mesh.shape["dp"] == 2
    in_specs = (
        P("dp", "tp", "ctx"),
        P("dp", "tp", "ctx"),
        P("dp", "tp", "ctx"),
        P("dp", ("ctx", "tp"), None),
        P("tp", "ctx", None),
        P("tp", None),
    )
    out_specs = (
        P("dp", "tp", "ctx"),
        P("dp", "tp", "ctx"),
        P("dp", "tp", "ctx"),
        P("tp", "ctx", "dp"),
    )
    return jax.shard_map(local, mesh=mesh, in_specs=in_specs, out_specs=out_specs, check_vma=False)
```

```python
import math

import jax
import jax.numpy as jnp
import numpy as np
from jax import lax
from jax.experimental import pallas as pl
from jax.experimental.pallas import tpu as pltpu
from jax.sharding import PartitionSpec as P

BF = jnp.bfloat16
F32 = jnp.float32


def angle(rows, cols, modulus):
    product = np.arange(rows)[:, None] * np.arange(cols)[None, :] % modulus
    return product.astype(np.float32) * np.float32(2.0 * math.pi / modulus)


def make_tables(block_rows, local_len, factor):
    half = block_rows // 2
    kept = half + 1
    rows = -(-kept // 16) * 16
    real = (np.arange(rows) < kept).astype(np.float32)[:, None]
    weight = np.where((np.arange(rows) == 0) | (np.arange(rows) == half), 1.0, 2.0)[:, None] * real
    fwd = angle(rows, half, block_rows)
    fwd_rows = np.concatenate([np.cos(fwd) * real, -np.sin(fwd) * real], axis=0)
    back_rows = np.concatenate([np.cos(fwd) * weight, -np.sin(fwd) * weight], axis=0).T * factor
    twid = angle(rows, local_len, block_rows * local_len)
    small = angle(local_len, local_len, local_len)
    c, s = np.cos(small), -np.sin(small)
    mat_fwd = np.block([[c, s], [-s, c]])
    mat_inv = np.block([[c, -s], [s, c]])
    pair = lambda a: np.concatenate([a, a], axis=1)
    return (
        jnp.asarray(fwd_rows, BF),
        jnp.asarray(back_rows, BF),
        jnp.asarray(pair(np.cos(twid)), F32),
        jnp.asarray(pair(-np.sin(twid)), F32),
        jnp.asarray(mat_fwd, BF),
        jnp.asarray(mat_inv, BF),
    )


def dot(a, b):
    return jnp.dot(a, b, preferred_element_type=F32)


def forward(blocks, fwd, tcos, tsin, mat, mixed):
    rows = fwd.shape[0] // 2
    n = blocks[0].shape[-1]
    tc, ts = tcos[...], tsin[...]
    for c in range(0, len(blocks), 2):
        a = dot(fwd[...], jnp.concatenate(blocks[c : c + 2], axis=-1))
        ar, ai = a[:rows], a[rows:]
        re = (ar * tc - ai * ts).astype(BF)
        im = (ar * ts + ai * tc).astype(BF)
        for j in range(2):
            at = pl.ds((c + j) * rows, rows)
            mixed[at, :n] = re[:, j * n : (j + 1) * n]
            mixed[at, n:] = im[:, j * n : (j + 1) * n]
    return dot(mixed[...], mat[...])


def join(re, im):
    return jnp.concatenate([re, im], axis=-1).astype(BF)


def inverse(joined, back, tcos, tsin, mat):
    rows = back.shape[1] // 2
    n = joined.shape[-1] // 2
    tc, ts = tcos[...], tsin[...]
    e = dot(joined, mat[...])
    out = []
    for c in range(0, e.shape[0], 2 * rows):
        e0, e1 = e[c : c + rows], e[c + rows : c + 2 * rows]
        er = jnp.concatenate([e0[:, :n], e1[:, :n]], axis=-1)
        ei = jnp.concatenate([e0[:, n:], e1[:, n:]], axis=-1)
        g = jnp.concatenate([er * tc + ei * ts, ei * tc - er * ts], axis=0).astype(BF)
        o = dot(back[...], g)
        out += [o[:, :n], o[:, n:]]
    return out


def split(spec):
    n = spec.shape[-1] // 2
    return spec[:, :n], spec[:, n:]


def by_channel(a):
    a = jnp.swapaxes(a.astype(F32), 0, 1).astype(BF)
    return [a[c] for c in range(a.shape[0])]


def by_block(parts):
    return jnp.swapaxes(jnp.stack(parts), 0, 1).astype(BF)


def cut_kernel(rows, out):
    out[0] = rows[...]


def pack_kernel(rows, q, k, v, packed, tokens):
    g = rows[...].astype(F32).T
    tokens[...] = g.astype(BF)
    shape = (packed.shape[0],) + packed.shape[2:]
    packed[:, 0] = (k[...].astype(F32) * v[...].astype(F32)).astype(BF).reshape(shape)
    packed[:, 1] = (g * q[...].astype(F32)).astype(BF).reshape(shape)


def filter_kernel(taps, fwd, tc, ts, mf, f_spec, mixed):
    f_spec[...] = forward([taps[c] for c in range(taps.shape[0])], fwd, tc, ts, mf, mixed)


def main_kernel(got, f_spec, fwd, back, tc, ts, mf, mi, both, lag_spec, mixed):
    fr, fi = split(f_spec[...])
    xr, xi = split(forward(by_channel(got[:, 0]), fwd, tc, ts, mf, mixed))
    both[:, 0] = by_block(inverse(join(fr * xr - fi * xi, fr * xi + fi * xr), back, tc, ts, mi))
    gr, gi = split(forward(by_channel(got[:, 1]), fwd, tc, ts, mf, mixed))
    lag_spec[...] = join(xr * gr + xi * gi, xr * gi - xi * gr)
    both[:, 1] = by_block(inverse(join(fr * gr + fi * gi, fr * gi - fi * gr), back, tc, ts, mi))


def out_kernel(both, packed, tokens, k, v, skip, query_out, key_out, value_out):
    shape = tokens.shape
    conv, corr = (both[:, i].astype(F32).reshape(shape) for i in range(2))
    gated, grad = (packed[:, i].astype(F32).reshape(shape) for i in range(2))
    s = skip[...]
    query_out[...] = (tokens[...].astype(F32) * (conv + s * gated)).astype(BF)
    total = corr + s * grad
    key_out[...] = (total * v[...].astype(F32)).astype(BF)
    value_out[...] = (total * k[...].astype(F32)).astype(BF)


def lag_kernel(lag_spec, own_rows, away_rows, tc, ts, mi, own, away):
    rows = own_rows.shape[0]
    both = jnp.concatenate([own_rows[...], away_rows[...]], axis=0)
    parts = inverse(lag_spec[...], both, tc, ts, mi)
    for c, part in enumerate(parts):
        own[c] = part[:rows]
        away[c] = part[rows:].astype(BF)


def call(body, grid, ins, tables, outs, vmem, mixed=None, placed=None):
    hbm = lambda a: a if a is placed else pltpu.with_memory_space_constraint(a, pltpu.HBM)

    def cut(a, dim):
        block = tuple(s // grid if i == dim else s for i, s in enumerate(a.shape))
        return pl.BlockSpec(block, lambda g: tuple(g if i == dim else 0 for i in range(len(block))))

    def whole(a):
        return pl.BlockSpec(a.shape, lambda g: (0,) * len(a.shape))

    return pl.pallas_call(
        body,
        grid=(grid,),
        in_specs=[cut(a, d) for a, d in ins] + [whole(a) for a in tables],
        out_specs=[cut(a, d) for a, d in outs],
        out_shape=[pltpu.HBM(a.shape, a.dtype) for a, _ in outs],
        scratch_shapes=[] if mixed is None else [pltpu.VMEM(mixed, BF)],
        compiler_params=pltpu.CompilerParams(vmem_limit_bytes=vmem * 2**20),
        cost_estimate=pl.CostEstimate(flops=2**20, bytes_accessed=2**20, transcendentals=0),
    )(*[hbm(a) for a, _ in ins], *[hbm(a) for a in tables])


def local(query_proj, key_proj, value_proj, out_grad, filter_taps, skip_gain):
    ctx = lax.axis_size("ctx")
    tp = lax.axis_size("tp")
    dp = lax.axis_size("dp")
    q, k, v = query_proj[0], key_proj[0], value_proj[0]
    chans, block = q.shape
    own = chans // ctx
    factor = 1.0 / (2 * ctx * block)
    fwd, back, tc, ts, mf, mi = make_tables(2 * ctx, block, factor)
    core = lax.axis_index("dp")
    struct = jax.ShapeDtypeStruct
    spec = struct((own * tc.shape[0], 2 * block), F32)
    mixed = (spec.shape[0] // 2, 2 * block)
    packed_type = struct((ctx, 2, own, block), BF)
    chan_type = struct((chans, block), BF)

    def exchange(a):
        flat = a.reshape(ctx, 2 * own, block)
        return lax.all_to_all(flat, "ctx", split_axis=0, concat_axis=0, tiled=True).reshape(a.shape)

    rows = out_grad[0]
    (cuts,) = call(
        cut_kernel, tp, [(rows, 1)], (), [(struct((tp, rows.shape[0], chans), BF), 0)], 16
    )
    rows = lax.all_to_all(cuts, "tp", split_axis=0, concat_axis=0, tiled=True)
    rows = rows.reshape(block, chans)
    packed, tokens = call(
        pack_kernel, 4, [(rows, 1), (q, 0), (k, 0), (v, 0)], (),
        [(packed_type, 0), (chan_type, 0)], 16,
    )
    got = exchange(packed)

    taps = filter_taps[0].reshape(own, ctx, block)
    (f_spec,) = call(filter_kernel, 2, [(taps, 0)], (fwd, tc, ts, mf), [(spec, 0)], 20, mixed)
    both, lag_spec = call(
        main_kernel, 2, [(got, 2), (f_spec, 0)], (fwd, back, tc, ts, mf, mi),
        [(packed_type, 2), (struct(spec.shape, BF), 0)], 32, mixed, got,
    )
    both = exchange(both)

    halves = back.reshape(dp, ctx // dp, -1)
    half_out = (own, ctx // dp, block)
    lag_own, lag_away = call(
        lag_kernel, 2, [(lag_spec, 0)],
        (
            lax.dynamic_index_in_dim(halves, core, keepdims=False),
            lax.dynamic_index_in_dim(halves, lax.rem(core + 1, dp), keepdims=False),
            tc, ts, mi,
        ),
        [(struct(half_out, F32), 0), (struct(half_out, BF), 0)], 28,
    )
    skip = jnp.broadcast_to(skip_gain[0][:, None], (chans, block))
    lag_away, skip = lax.optimization_barrier((lag_away, skip))
    other = lax.ppermute(lag_away, "dp", [(j, (j + 1) % dp) for j in range(dp)])
    grad_scale = 1.0 / math.sqrt(dp * ctx * block)
    filter_out = ((lag_own + other.astype(F32)) * grad_scale).reshape(1, own, -1)

    query_out, key_out, value_out = call(
        out_kernel, 4, [(both, 0), (packed, 0), (tokens, 0), (k, 0), (v, 0), (skip, 0)], (),
        [(chan_type, 0)] * 3, 16, placed=both,
    )
    return (query_out[None], key_out[None], value_out[None], filter_out)


def solution(mesh):
    assert mesh.shape["dp"] == 2
    in_specs = (
        P("dp", "tp", "ctx"),
        P("dp", "tp", "ctx"),
        P("dp", "tp", "ctx"),
        P("dp", ("ctx", "tp"), None),
        P("tp", "ctx", None),
        P("tp", None),
    )
    out_specs = (
        P("dp", "tp", "ctx"),
        P("dp", "tp", "ctx"),
        P("dp", "tp", "ctx"),
        P("tp", "ctx", "dp"),
    )
    return jax.shard_map(local, mesh=mesh, in_specs=in_specs, out_specs=out_specs, check_vma=False)
```

```python
import math

import jax
import jax.numpy as jnp
import numpy as np
from jax import lax
from jax.experimental import pallas as pl
from jax.experimental.pallas import tpu as pltpu
from jax.sharding import PartitionSpec as P

BF = jnp.bfloat16
F32 = jnp.float32


def angle(rows, cols, modulus):
    product = np.arange(rows)[:, None] * np.arange(cols)[None, :] % modulus
    return product.astype(np.float32) * np.float32(2.0 * math.pi / modulus)


def make_tables(block_rows, local_len, factor):
    half = block_rows // 2
    kept = half + 1
    rows = -(-kept // 16) * 16
    real = (np.arange(rows) < kept).astype(np.float32)[:, None]
    weight = np.where((np.arange(rows) == 0) | (np.arange(rows) == half), 1.0, 2.0)[:, None] * real
    fwd = angle(rows, half, block_rows)
    fwd_rows = np.concatenate([np.cos(fwd) * real, -np.sin(fwd) * real], axis=0)
    back_rows = np.concatenate([np.cos(fwd) * weight, -np.sin(fwd) * weight], axis=0).T * factor
    twid = angle(rows, local_len, block_rows * local_len)
    small = angle(local_len, local_len, local_len)
    c, s = np.cos(small), -np.sin(small)
    mat_fwd = np.block([[c, s], [-s, c]])
    mat_inv = np.block([[c, -s], [s, c]])
    pair = lambda a: np.concatenate([a, a], axis=1)
    return (
        jnp.asarray(fwd_rows, BF),
        jnp.asarray(back_rows, BF),
        jnp.asarray(pair(np.cos(twid)), F32),
        jnp.asarray(pair(-np.sin(twid)), F32),
        jnp.asarray(mat_fwd, BF),
        jnp.asarray(mat_inv, BF),
    )


def dot(a, b):
    return jnp.dot(a, b, preferred_element_type=F32)


def forward(blocks, fwd, tcos, tsin, mat, mixed):
    rows = fwd.shape[0] // 2
    n = blocks[0].shape[-1]
    tc, ts = tcos[...], tsin[...]
    for c in range(0, len(blocks), 2):
        a = dot(fwd[...], jnp.concatenate(blocks[c : c + 2], axis=-1))
        ar, ai = a[:rows], a[rows:]
        re = (ar * tc - ai * ts).astype(BF)
        im = (ar * ts + ai * tc).astype(BF)
        for j in range(2):
            at = pl.ds((c + j) * rows, rows)
            mixed[at, :n] = re[:, j * n : (j + 1) * n]
            mixed[at, n:] = im[:, j * n : (j + 1) * n]
    return dot(mixed[...], mat[...])


def join(re, im):
    return jnp.concatenate([re, im], axis=-1).astype(BF)


def inverse(joined, back, tcos, tsin, mat):
    rows = back.shape[1] // 2
    n = joined.shape[-1] // 2
    tc, ts = tcos[...], tsin[...]
    e = dot(joined, mat[...])
    out = []
    for c in range(0, e.shape[0], 2 * rows):
        e0, e1 = e[c : c + rows], e[c + rows : c + 2 * rows]
        er = jnp.concatenate([e0[:, :n], e1[:, :n]], axis=-1)
        ei = jnp.concatenate([e0[:, n:], e1[:, n:]], axis=-1)
        g = jnp.concatenate([er * tc + ei * ts, ei * tc - er * ts], axis=0).astype(BF)
        o = dot(back[...], g)
        out += [o[:, :n], o[:, n:]]
    return out


def split(spec):
    n = spec.shape[-1] // 2
    return spec[:, :n], spec[:, n:]


def by_channel(a):
    a = jnp.swapaxes(a.astype(F32), 0, 1).astype(BF)
    return [a[c] for c in range(a.shape[0])]


def by_block(parts):
    return jnp.swapaxes(jnp.stack(parts), 0, 1).astype(BF)


def cut_kernel(rows, out, sems):
    width = out.shape[2]
    copies = [
        pltpu.make_async_copy(rows.at[:, pl.ds(i * width, width)], out.at[i], sems.at[i])
        for i in range(out.shape[0])
    ]
    for copy in copies:
        copy.start()
    for copy in copies:
        copy.wait()


def gated_kernel(k, v, packed):
    shape = (packed.shape[0],) + packed.shape[2:]
    packed[:, 0] = (k[...].astype(F32) * v[...].astype(F32)).astype(BF).reshape(shape)


def grad_kernel(rows, q, half_packed, packed):
    shape = (packed.shape[0],) + packed.shape[2:]
    packed[:, 0] = (rows[...].astype(F32).T * q[...].astype(F32)).astype(BF).reshape(shape)


def tokens_kernel(rows, tokens):
    tokens[...] = rows[...].astype(F32).T.astype(BF)


def filter_kernel(taps, fwd, tc, ts, mf, f_spec, mixed):
    f_spec[...] = forward([taps[c] for c in range(taps.shape[0])], fwd, tc, ts, mf, mixed)


def main_kernel(got, f_spec, fwd, back, tc, ts, mf, mi, both, lag_spec, mixed):
    fr, fi = split(f_spec[...])
    xr, xi = split(forward(by_channel(got[:, 0]), fwd, tc, ts, mf, mixed))
    both[:, 0] = by_block(inverse(join(fr * xr - fi * xi, fr * xi + fi * xr), back, tc, ts, mi))
    gr, gi = split(forward(by_channel(got[:, 1]), fwd, tc, ts, mf, mixed))
    lag_spec[...] = join(xr * gr + xi * gi, xr * gi - xi * gr)
    both[:, 1] = by_block(inverse(join(fr * gr + fi * gi, fr * gi - fi * gr), back, tc, ts, mi))


def out_kernel(both, packed, tokens, k, v, skip, query_out, key_out, value_out):
    shape = tokens.shape
    s = lax.broadcast_in_dim(skip[...], skip.shape + (shape[1],), (0, 1))
    conv, corr = (both[:, i].astype(F32) for i in range(2))
    gated, grad = (packed[:, i].astype(F32) for i in range(2))
    through = (conv + s * gated).reshape(shape)
    query_out[...] = (tokens[...].astype(F32) * through).astype(BF)
    total = (corr + s * grad).reshape(shape)
    key_out[...] = (total * v[...].astype(F32)).astype(BF)
    value_out[...] = (total * k[...].astype(F32)).astype(BF)


def lag_kernel(lag_spec, own_rows, away_rows, tc, ts, mi, own, away):
    rows = own_rows.shape[0]
    both = jnp.concatenate([own_rows[...], away_rows[...]], axis=0)
    parts = inverse(lag_spec[...], both, tc, ts, mi)
    for c, part in enumerate(parts):
        own[c] = part[:rows]
        away[c] = part[rows:].astype(BF)


def hbm(a):
    return pltpu.with_memory_space_constraint(a, pltpu.HBM)


def hbm_out(a):
    return pltpu.HBM(a.shape, a.dtype)


def cut(a, dim, grid, at=None):
    block = [s // grid if i == dim else s for i, s in enumerate(a.shape)]
    index = [0] * len(block)
    if at:
        block[at[0]], index[at[0]] = 1, at[1]
    return pl.BlockSpec(
        tuple(block), lambda g: tuple(g if i == dim else n for i, n in enumerate(index))
    )


def call(body, grid, ins, tables, outs, vmem, mixed=None):
    return pl.pallas_call(
        body,
        grid=(grid,),
        in_specs=[cut(a, d, grid) for a, d in ins] + [cut(a, None, grid) for a in tables],
        out_specs=[cut(a, d, grid) for a, d in outs],
        out_shape=[a for a, _ in outs],
        scratch_shapes=[] if mixed is None else [pltpu.VMEM(mixed, BF)],
        compiler_params=pltpu.CompilerParams(vmem_limit_bytes=vmem * 2**20),
        cost_estimate=pl.CostEstimate(flops=2**20, bytes_accessed=2**20, transcendentals=0),
    )(*[a for a, _ in ins], *[hbm(a) for a in tables])


def local(query_proj, key_proj, value_proj, out_grad, filter_taps, skip_gain):
    ctx = lax.axis_size("ctx")
    tp = lax.axis_size("tp")
    dp = lax.axis_size("dp")
    q, k, v = query_proj[0], key_proj[0], value_proj[0]
    chans, block = q.shape
    own = chans // ctx
    factor = 1.0 / (2 * ctx * block)
    fwd, back, tc, ts, mf, mi = make_tables(2 * ctx, block, factor)
    core = lax.axis_index("dp")
    struct = jax.ShapeDtypeStruct
    spec = struct((own * tc.shape[0], 2 * block), F32)
    mixed = (spec.shape[0] // 2, 2 * block)
    packed_type = struct((ctx, 2, own, block), BF)
    chan_type = struct((chans, block), BF)

    def exchange(a):
        flat = a.reshape(ctx, 2 * own, block)
        return lax.all_to_all(flat, "ctx", split_axis=0, concat_axis=0, tiled=True).reshape(a.shape)

    rows = out_grad[0]
    anywhere = pl.BlockSpec(memory_space=pl.ANY)
    cuts = pl.pallas_call(
        cut_kernel,
        in_specs=[anywhere],
        out_specs=anywhere,
        out_shape=pltpu.HBM((tp, rows.shape[0], chans), BF),
        scratch_shapes=[pltpu.SemaphoreType.DMA((tp,))],
    )(hbm(rows))
    rows = lax.all_to_all(cuts, "tp", split_axis=0, concat_axis=0, tiled=True)
    rows = rows.reshape(block, chans)

    grid = 4
    params = pltpu.CompilerParams(vmem_limit_bytes=16 * 2**20)
    half_packed = pl.pallas_call(
        gated_kernel,
        grid=(grid,),
        in_specs=[cut(k, 0, grid), cut(v, 0, grid)],
        out_specs=cut(packed_type, 0, grid, (1, 0)),
        out_shape=hbm_out(packed_type),
        compiler_params=params,
    )(hbm(k), hbm(v))
    packed = pl.pallas_call(
        grad_kernel,
        grid=(grid,),
        in_specs=[cut(rows, 1, grid), cut(q, 0, grid), anywhere],
        out_specs=cut(packed_type, 0, grid, (1, 1)),
        out_shape=hbm_out(packed_type),
        input_output_aliases={2: 0},
        compiler_params=params,
    )(rows, hbm(q), hbm(half_packed))
    (tokens,) = call(tokens_kernel, grid, [(rows, 1)], (), [(hbm_out(chan_type), 0)], 16)
    got = exchange(packed)

    taps = filter_taps[0].reshape(own, ctx, block)
    (f_spec,) = call(filter_kernel, 2, [(taps, 0)], (fwd, tc, ts, mf), [(spec, 0)], 20, mixed)
    both, lag_spec = call(
        main_kernel, 2, [(got, 2), (f_spec, 0)], (fwd, back, tc, ts, mf, mi),
        [(hbm_out(packed_type), 2), (hbm_out(struct(spec.shape, BF)), 0)], 32, mixed,
    )
    both = exchange(both)

    halves = back.reshape(dp, ctx // dp, -1)
    half_out = (own, ctx // dp, block)
    lag_own, lag_away = call(
        lag_kernel, 2, [(lag_spec, 0)],
        (
            lax.dynamic_index_in_dim(halves, core, keepdims=False),
            lax.dynamic_index_in_dim(halves, lax.rem(core + 1, dp), keepdims=False),
            tc, ts, mi,
        ),
        [(struct(half_out, F32), 0), (struct(half_out, BF), 0)], 28,
    )
    other = lax.ppermute(lag_away, "dp", [(j, (j + 1) % dp) for j in range(dp)])
    grad_scale = 1.0 / math.sqrt(dp * ctx * block)
    filter_out = ((lag_own + other.astype(F32)) * grad_scale).reshape(1, own, -1)

    query_out, key_out, value_out = call(
        out_kernel, grid,
        [(both, 0), (packed, 0), (tokens, 0), (hbm(k), 0), (hbm(v), 0), (skip_gain[0].reshape(ctx, own), 0)],
        (), [(hbm_out(chan_type), 0)] * 3, 16,
    )
    return (query_out[None], key_out[None], value_out[None], filter_out)


def solution(mesh):
    assert mesh.shape["dp"] == 2
    in_specs = (
        P("dp", "tp", "ctx"),
        P("dp", "tp", "ctx"),
        P("dp", "tp", "ctx"),
        P("dp", ("ctx", "tp"), None),
        P("tp", "ctx", None),
        P("tp", None),
    )
    out_specs = (
        P("dp", "tp", "ctx"),
        P("dp", "tp", "ctx"),
        P("dp", "tp", "ctx"),
        P("tp", "ctx", "dp"),
    )
    return jax.shard_map(local, mesh=mesh, in_specs=in_specs, out_specs=out_specs, check_vma=False)
```

```python
import functools
import math

import jax
import jax.numpy as jnp
import numpy as np
from jax import lax
from jax.experimental import pallas as pl
from jax.experimental.pallas import tpu as pltpu
from jax.sharding import PartitionSpec as P

BF = jnp.bfloat16
F32 = jnp.float32


def angle(rows, cols, modulus):
    product = np.arange(rows)[:, None] * np.arange(cols)[None, :] % modulus
    return product.astype(np.float32) * np.float32(2.0 * math.pi / modulus)


def make_tables(block_rows, local_len, factor):
    half = block_rows // 2
    kept = half + 1
    rows = -(-kept // 16) * 16
    real = (np.arange(rows) < kept).astype(np.float32)[:, None]
    weight = np.where((np.arange(rows) == 0) | (np.arange(rows) == half), 1.0, 2.0)[:, None] * real
    fwd = angle(rows, half, block_rows)
    fwd_rows = np.concatenate([np.cos(fwd) * real, -np.sin(fwd) * real], axis=0)
    back_rows = np.concatenate([np.cos(fwd) * weight, -np.sin(fwd) * weight], axis=0).T * factor
    twid = angle(rows, local_len, block_rows * local_len)
    small = angle(local_len, local_len, local_len)
    c, s = np.cos(small), -np.sin(small)
    mat_fwd = np.block([[c, s], [-s, c]])
    mat_inv = np.block([[c, -s], [s, c]])
    pair = lambda a: np.concatenate([a, a], axis=1)
    return (
        jnp.asarray(fwd_rows, BF),
        jnp.asarray(back_rows, BF),
        jnp.asarray(pair(np.cos(twid)), F32),
        jnp.asarray(pair(-np.sin(twid)), F32),
        jnp.asarray(mat_fwd, BF),
        jnp.asarray(mat_inv, BF),
    )


def dot(a, b):
    return jnp.dot(a, b, preferred_element_type=F32)


def forward(blocks, fwd, tcos, tsin, mat, mixed):
    rows = fwd.shape[0] // 2
    n = blocks[0].shape[-1]
    tc, ts = tcos[...], tsin[...]
    for c in range(0, len(blocks), 2):
        a = dot(fwd[...], jnp.concatenate(blocks[c : c + 2], axis=-1))
        ar, ai = a[:rows], a[rows:]
        re = (ar * tc - ai * ts).astype(BF)
        im = (ar * ts + ai * tc).astype(BF)
        for j in range(2):
            at = pl.ds((c + j) * rows, rows)
            mixed[at, :n] = re[:, j * n : (j + 1) * n]
            mixed[at, n:] = im[:, j * n : (j + 1) * n]
    return dot(mixed[...], mat[...])


def join(re, im):
    return jnp.concatenate([re, im], axis=-1).astype(BF)


def inverse(joined, back, tcos, tsin, mat):
    rows = back.shape[1] // 2
    n = joined.shape[-1] // 2
    tc, ts = tcos[...], tsin[...]
    e = dot(joined, mat[...])
    out = []
    for c in range(0, e.shape[0], 2 * rows):
        e0, e1 = e[c : c + rows], e[c + rows : c + 2 * rows]
        er = jnp.concatenate([e0[:, :n], e1[:, :n]], axis=-1)
        ei = jnp.concatenate([e0[:, n:], e1[:, n:]], axis=-1)
        g = jnp.concatenate([er * tc + ei * ts, ei * tc - er * ts], axis=0).astype(BF)
        o = dot(back[...], g)
        out += [o[:, :n], o[:, n:]]
    return out


def split(spec):
    n = spec.shape[-1] // 2
    return spec[:, :n], spec[:, n:]


def by_channel(a):
    a = jnp.swapaxes(a.astype(F32), 0, 1).astype(BF)
    return [a[c] for c in range(a.shape[0])]


def by_block(parts):
    return jnp.swapaxes(jnp.stack(parts), 0, 1).astype(BF)


def cut_kernel(rows, out, held, sems):
    parts, count, width = out.shape
    half = count // 2
    ins, outs = [], []
    for i in range(parts):
        for j in range(2):
            at = pl.ds(j * half, half)
            n = 2 * i + j
            here = held.at[i, at]
            ins.append(
                pltpu.make_async_copy(rows.at[at, pl.ds(i * width, width)], here, sems.at[0, n])
            )
            outs.append(pltpu.make_async_copy(here, out.at[i, at], sems.at[1, n]))
    for copy in ins:
        copy.start()
    for copy, back in zip(ins, outs):
        copy.wait()
        back.start()
    for back in outs:
        back.wait()


def gated_kernel(k, v, q, packed, q_near):
    q_near[...] = q[...]
    shape = (packed.shape[0],) + packed.shape[2:]
    packed[:, 0] = (k[...].astype(F32) * v[...].astype(F32)).astype(BF).reshape(shape)


def grad_kernel(rows, q, half_packed, packed):
    shape = (packed.shape[0],) + packed.shape[2:]
    packed[:, 0] = (rows[...].astype(F32).T * q[...].astype(F32)).astype(BF).reshape(shape)


def tokens_kernel(rows, tokens):
    tokens[...] = rows[...].astype(F32).T.astype(BF)


def filter_kernel(taps, fwd, tc, ts, mf, f_spec, mixed):
    f_spec[...] = forward([taps[c] for c in range(taps.shape[0])], fwd, tc, ts, mf, mixed)


def main_kernel(got, f_spec, fwd, back, tc, ts, mf, mi, both, lag_spec, mixed):
    fr, fi = split(f_spec[...])
    xr, xi = split(forward(by_channel(got[:, 0]), fwd, tc, ts, mf, mixed))
    both[:, 0] = by_block(inverse(join(fr * xr - fi * xi, fr * xi + fi * xr), back, tc, ts, mi))
    gr, gi = split(forward(by_channel(got[:, 1]), fwd, tc, ts, mf, mixed))
    lag_spec[...] = join(xr * gr + xi * gi, xr * gi - xi * gr)
    both[:, 1] = by_block(inverse(join(fr * gr + fi * gi, fr * gi - fi * gr), back, tc, ts, mi))


def add_kernel(own, other, out, *, scale):
    total = jnp.swapaxes((own[...] + other[...].astype(F32)) * scale, 0, 1)
    n = total.shape[-1]
    for m in range(total.shape[0]):
        out[:, m * n : (m + 1) * n] = total[m]


def out_kernel(both, packed, tokens, k, v, skip, query_out, key_out, value_out):
    shape = tokens.shape
    s = lax.broadcast_in_dim(skip[...], skip.shape + (shape[1],), (0, 1))
    conv, corr = (both[:, i].astype(F32) for i in range(2))
    gated, grad = (packed[:, i].astype(F32) for i in range(2))
    through = (conv + s * gated).reshape(shape)
    query_out[...] = (tokens[...].astype(F32) * through).astype(BF)
    total = (corr + s * grad).reshape(shape)
    key_out[...] = (total * v[...].astype(F32)).astype(BF)
    value_out[...] = (total * k[...].astype(F32)).astype(BF)


def lag_kernel(lag_spec, own_rows, away_rows, tc, ts, mi, own, away):
    rows = own_rows.shape[0]
    both = jnp.concatenate([own_rows[...], away_rows[...]], axis=0)
    parts = inverse(lag_spec[...], both, tc, ts, mi)
    for c, part in enumerate(parts):
        own[c] = part[:rows]
        away[c] = part[rows:].astype(BF)


def hbm(a):
    return pltpu.with_memory_space_constraint(a, pltpu.HBM)


def hbm_out(a):
    return pltpu.HBM(a.shape, a.dtype)


def vmem(a):
    return pltpu.with_memory_space_constraint(a, pltpu.VMEM)


def vmem_out(a):
    return pltpu.VMEM(a.shape, a.dtype)


def cut(a, dim, grid, at=None):
    block = [s // grid if i == dim else s for i, s in enumerate(a.shape)]
    index = [0] * len(block)
    if at:
        block[at[0]], index[at[0]] = 1, at[1]
    return pl.BlockSpec(
        tuple(block), lambda g: tuple(g if i == dim else n for i, n in enumerate(index))
    )


def call(body, grid, ins, tables, outs, vmem, mixed=None):
    return pl.pallas_call(
        body,
        grid=(grid,),
        in_specs=[cut(a, d, grid) for a, d in ins] + [cut(a, None, grid) for a in tables],
        out_specs=[cut(a, d, grid) for a, d in outs],
        out_shape=[a for a, _ in outs],
        scratch_shapes=[] if mixed is None else [pltpu.VMEM(mixed, BF)],
        compiler_params=pltpu.CompilerParams(vmem_limit_bytes=vmem * 2**20),
        cost_estimate=pl.CostEstimate(flops=2**20, bytes_accessed=2**20, transcendentals=0),
    )(*[a for a, _ in ins], *[hbm(a) for a in tables])


def local(query_proj, key_proj, value_proj, out_grad, filter_taps, skip_gain):
    ctx = lax.axis_size("ctx")
    tp = lax.axis_size("tp")
    dp = lax.axis_size("dp")
    q, k, v = query_proj[0], key_proj[0], value_proj[0]
    chans, block = q.shape
    own = chans // ctx
    factor = 1.0 / (2 * ctx * block)
    fwd, back, tc, ts, mf, mi = make_tables(2 * ctx, block, factor)
    core = lax.axis_index("dp")
    struct = jax.ShapeDtypeStruct
    spec = struct((own * tc.shape[0], 2 * block), F32)
    mixed = (spec.shape[0] // 2, 2 * block)
    packed_type = struct((ctx, 2, own, block), BF)
    chan_type = struct((chans, block), BF)

    def exchange(a):
        flat = a.reshape(ctx, 2 * own, block)
        return lax.all_to_all(flat, "ctx", split_axis=0, concat_axis=0, tiled=True).reshape(a.shape)

    rows = out_grad[0]
    anywhere = pl.BlockSpec(memory_space=pl.ANY)
    cuts = pl.pallas_call(
        cut_kernel,
        in_specs=[anywhere],
        out_specs=anywhere,
        out_shape=pltpu.HBM((tp, rows.shape[0], chans), BF),
        scratch_shapes=[
            pltpu.VMEM((tp, rows.shape[0], chans), BF),
            pltpu.SemaphoreType.DMA((2, 2 * tp)),
        ],
    )(hbm(rows))
    rows = lax.all_to_all(cuts, "tp", split_axis=0, concat_axis=0, tiled=True)
    rows = rows.reshape(block, chans)

    grid = 4
    params = pltpu.CompilerParams(vmem_limit_bytes=16 * 2**20)
    half_packed, q_near = pl.pallas_call(
        gated_kernel,
        grid=(grid,),
        in_specs=[cut(k, 0, grid), cut(v, 0, grid), cut(q, 0, grid)],
        out_specs=[cut(packed_type, 0, grid, (1, 0)), cut(q, 0, grid)],
        out_shape=[hbm_out(packed_type), vmem_out(q)],
        compiler_params=params,
    )(hbm(k), hbm(v), hbm(q))
    packed = pl.pallas_call(
        grad_kernel,
        grid=(grid,),
        in_specs=[cut(rows, 1, grid), cut(q, 0, grid), anywhere],
        out_specs=cut(packed_type, 0, grid, (1, 1)),
        out_shape=hbm_out(packed_type),
        input_output_aliases={2: 0},
        compiler_params=params,
    )(rows, vmem(q_near), hbm(half_packed))
    got = exchange(packed)

    taps = filter_taps[0].reshape(own, ctx, block)
    (f_spec,) = call(filter_kernel, 2, [(taps, 0)], (fwd, tc, ts, mf), [(spec, 0)], 20, mixed)
    both, lag_spec = call(
        main_kernel, 2, [(got, 2), (f_spec, 0)], (fwd, back, tc, ts, mf, mi),
        [(hbm_out(packed_type), 2), (hbm_out(struct(spec.shape, BF)), 0)], 32, mixed,
    )
    both = exchange(both)

    halves = back.reshape(dp, ctx // dp, -1)
    half_out = (own, ctx // dp, block)
    lag_own, lag_away = call(
        lag_kernel, 2, [(lag_spec, 0)],
        (
            lax.dynamic_index_in_dim(halves, core, keepdims=False),
            lax.dynamic_index_in_dim(halves, lax.rem(core + 1, dp), keepdims=False),
            tc, ts, mi,
        ),
        [(struct(half_out, F32), 0), (struct(half_out, BF), 0)], 28,
    )
    lag_away, rows = lax.optimization_barrier((lag_away, rows))
    other = lax.ppermute(lag_away, "dp", [(j, (j + 1) % dp) for j in range(dp)])
    grad_scale = 1.0 / math.sqrt(dp * ctx * block)
    (filter_out,) = call(
        functools.partial(add_kernel, scale=grad_scale), 2, [(lag_own, 0), (other, 0)], (),
        [(hbm_out(struct((own, ctx * block // dp), F32)), 0)], 16,
    )

    (tokens,) = call(tokens_kernel, grid, [(rows, 1)], (), [(hbm_out(chan_type), 0)], 16)
    query_out, key_out, value_out = call(
        out_kernel, grid,
        [(both, 0), (packed, 0), (hbm(tokens), 0), (hbm(k), 0), (hbm(v), 0), (skip_gain[0].reshape(ctx, own), 0)],
        (), [(hbm_out(chan_type), 0)] * 3, 16,
    )
    return (query_out[None], key_out[None], value_out[None], filter_out[None])


def solution(mesh):
    assert mesh.shape["dp"] == 2
    in_specs = (
        P("dp", "tp", "ctx"),
        P("dp", "tp", "ctx"),
        P("dp", "tp", "ctx"),
        P("dp", ("ctx", "tp"), None),
        P("tp", "ctx", None),
        P("tp", None),
    )
    out_specs = (
        P("dp", "tp", "ctx"),
        P("dp", "tp", "ctx"),
        P("dp", "tp", "ctx"),
        P("tp", "ctx", "dp"),
    )
    return jax.shard_map(local, mesh=mesh, in_specs=in_specs, out_specs=out_specs, check_vma=False)
```

```python
import functools
import math

import jax
import jax.numpy as jnp
import numpy as np
from jax import lax
from jax.experimental import pallas as pl
from jax.experimental.pallas import tpu as pltpu
from jax.sharding import PartitionSpec as P

BF = jnp.bfloat16
F32 = jnp.float32


def angle(rows, cols, modulus):
    product = np.arange(rows)[:, None] * np.arange(cols)[None, :] % modulus
    return product.astype(np.float32) * np.float32(2.0 * math.pi / modulus)


def make_tables(block_rows, local_len, factor):
    half = block_rows // 2
    kept = half + 1
    rows = -(-kept // 16) * 16
    real = (np.arange(rows) < kept).astype(np.float32)[:, None]
    weight = np.where((np.arange(rows) == 0) | (np.arange(rows) == half), 1.0, 2.0)[:, None] * real
    fwd = angle(rows, half, block_rows)
    fwd_rows = np.concatenate([np.cos(fwd) * real, -np.sin(fwd) * real], axis=0)
    back_rows = np.concatenate([np.cos(fwd) * weight, -np.sin(fwd) * weight], axis=0).T * factor
    twid = angle(rows, local_len, block_rows * local_len)
    small = angle(local_len, local_len, local_len)
    c, s = np.cos(small), -np.sin(small)
    mat_fwd = np.block([[c, s], [-s, c]])
    mat_inv = np.block([[c, -s], [s, c]])
    pair = lambda a: np.concatenate([a, a], axis=1)
    return (
        jnp.asarray(fwd_rows, BF),
        jnp.asarray(back_rows, BF),
        jnp.asarray(pair(np.cos(twid)), F32),
        jnp.asarray(pair(-np.sin(twid)), F32),
        jnp.asarray(mat_fwd, BF),
        jnp.asarray(mat_inv, BF),
    )


def dot(a, b):
    return jnp.dot(a, b, preferred_element_type=F32)


def forward(blocks, fwd, tcos, tsin, mat, mixed):
    rows = fwd.shape[0] // 2
    n = blocks[0].shape[-1]
    tc, ts = tcos[...], tsin[...]
    for c in range(0, len(blocks), 2):
        a = dot(fwd[...], jnp.concatenate(blocks[c : c + 2], axis=-1))
        ar, ai = a[:rows], a[rows:]
        re = (ar * tc - ai * ts).astype(BF)
        im = (ar * ts + ai * tc).astype(BF)
        for j in range(2):
            at = pl.ds((c + j) * rows, rows)
            mixed[at, :n] = re[:, j * n : (j + 1) * n]
            mixed[at, n:] = im[:, j * n : (j + 1) * n]
    return dot(mixed[...], mat[...])


def join(re, im):
    return jnp.concatenate([re, im], axis=-1).astype(BF)


def inverse(joined, back, tcos, tsin, mat):
    rows = back.shape[1] // 2
    n = joined.shape[-1] // 2
    tc, ts = tcos[...], tsin[...]
    e = dot(joined, mat[...])
    out = []
    for c in range(0, e.shape[0], 2 * rows):
        e0, e1 = e[c : c + rows], e[c + rows : c + 2 * rows]
        er = jnp.concatenate([e0[:, :n], e1[:, :n]], axis=-1)
        ei = jnp.concatenate([e0[:, n:], e1[:, n:]], axis=-1)
        g = jnp.concatenate([er * tc + ei * ts, ei * tc - er * ts], axis=0).astype(BF)
        o = dot(back[...], g)
        out += [o[:, :n], o[:, n:]]
    return out


def split(spec):
    n = spec.shape[-1] // 2
    return spec[:, :n], spec[:, n:]


def by_channel(a):
    a = jnp.swapaxes(a.astype(F32), 0, 1).astype(BF)
    return [a[c] for c in range(a.shape[0])]


def by_block(parts):
    return jnp.swapaxes(jnp.stack(parts), 0, 1).astype(BF)


def cut_kernel(rows, out, held, sems):
    parts, count, width = out.shape
    half = count // 2
    ins, outs = [], []
    for i in range(parts):
        for j in range(2):
            at = pl.ds(j * half, half)
            n = 2 * i + j
            here = held.at[i, at]
            ins.append(
                pltpu.make_async_copy(rows.at[at, pl.ds(i * width, width)], here, sems.at[0, n])
            )
            outs.append(pltpu.make_async_copy(here, out.at[i, at], sems.at[1, n]))
    for copy in ins:
        copy.start()
    for copy, back in zip(ins, outs):
        copy.wait()
        back.start()
    for back in outs:
        back.wait()


def gated_kernel(k, v, q, packed, q_near):
    q_near[...] = q[...]
    shape = (packed.shape[0],) + packed.shape[2:]
    packed[:, 0] = (k[...].astype(F32) * v[...].astype(F32)).astype(BF).reshape(shape)


def grad_kernel(rows, q, half_packed, packed):
    shape = (packed.shape[0],) + packed.shape[2:]
    packed[:, 0] = (rows[...].astype(F32).T * q[...].astype(F32)).astype(BF).reshape(shape)


def near_kernel(rows, k, v, near):
    near[0] = rows[...].astype(F32).T.astype(BF)
    near[1] = k[...]
    near[2] = v[...]


def filter_kernel(taps, fwd, tc, ts, mf, f_spec, mixed):
    f_spec[...] = forward([taps[c] for c in range(taps.shape[0])], fwd, tc, ts, mf, mixed)


def main_kernel(got, f_spec, fwd, back, tc, ts, mf, mi, both, lag_spec, mixed):
    fr, fi = split(f_spec[...])
    xr, xi = split(forward(by_channel(got[:, 0]), fwd, tc, ts, mf, mixed))
    both[:, 0] = by_block(inverse(join(fr * xr - fi * xi, fr * xi + fi * xr), back, tc, ts, mi))
    gr, gi = split(forward(by_channel(got[:, 1]), fwd, tc, ts, mf, mixed))
    lag_spec[...] = join(xr * gr + xi * gi, xr * gi - xi * gr)
    both[:, 1] = by_block(inverse(join(fr * gr + fi * gi, fr * gi - fi * gr), back, tc, ts, mi))


def add_kernel(own, other, out, *, scale):
    total = jnp.swapaxes((own[...] + other[...].astype(F32)) * scale, 0, 1)
    n = total.shape[-1]
    for m in range(total.shape[0]):
        out[:, m * n : (m + 1) * n] = total[m]


def out_kernel(both, packed, near, skip, query_out, key_out, value_out):
    shape = query_out.shape
    tokens, k, v = (near[i].astype(F32) for i in range(3))
    s = lax.broadcast_in_dim(skip[...], skip.shape + (shape[1],), (0, 1))
    conv, corr = (both[:, i].astype(F32) for i in range(2))
    gated, grad = (packed[:, i].astype(F32) for i in range(2))
    through = (conv + s * gated).reshape(shape)
    query_out[...] = (tokens * through).astype(BF)
    total = (corr + s * grad).reshape(shape)
    key_out[...] = (total * v).astype(BF)
    value_out[...] = (total * k).astype(BF)


def lag_kernel(lag_spec, own_rows, away_rows, tc, ts, mi, own, away):
    rows = own_rows.shape[0]
    both = jnp.concatenate([own_rows[...], away_rows[...]], axis=0)
    parts = inverse(lag_spec[...], both, tc, ts, mi)
    for c, part in enumerate(parts):
        own[c] = part[:rows]
        away[c] = part[rows:].astype(BF)


def hbm(a):
    return pltpu.with_memory_space_constraint(a, pltpu.HBM)


def hbm_out(a):
    return pltpu.HBM(a.shape, a.dtype)


def vmem(a):
    return pltpu.with_memory_space_constraint(a, pltpu.VMEM)


def vmem_out(a):
    return pltpu.VMEM(a.shape, a.dtype)


def cut(a, dim, grid, at=None):
    block = [s // grid if i == dim else s for i, s in enumerate(a.shape)]
    index = [0] * len(block)
    if at:
        block[at[0]], index[at[0]] = 1, at[1]
    return pl.BlockSpec(
        tuple(block), lambda g: tuple(g if i == dim else n for i, n in enumerate(index))
    )


def call(body, grid, ins, tables, outs, vmem, mixed=None):
    return pl.pallas_call(
        body,
        grid=(grid,),
        in_specs=[cut(a, d, grid) for a, d in ins] + [cut(a, None, grid) for a in tables],
        out_specs=[cut(a, d, grid) for a, d in outs],
        out_shape=[a for a, _ in outs],
        scratch_shapes=[] if mixed is None else [pltpu.VMEM(mixed, BF)],
        compiler_params=pltpu.CompilerParams(vmem_limit_bytes=vmem * 2**20),
        cost_estimate=pl.CostEstimate(flops=2**20, bytes_accessed=2**20, transcendentals=0),
    )(*[a for a, _ in ins], *[hbm(a) for a in tables])


def local(query_proj, key_proj, value_proj, out_grad, filter_taps, skip_gain):
    ctx = lax.axis_size("ctx")
    tp = lax.axis_size("tp")
    dp = lax.axis_size("dp")
    q, k, v = query_proj[0], key_proj[0], value_proj[0]
    chans, block = q.shape
    own = chans // ctx
    factor = 1.0 / (2 * ctx * block)
    fwd, back, tc, ts, mf, mi = make_tables(2 * ctx, block, factor)
    core = lax.axis_index("dp")
    struct = jax.ShapeDtypeStruct
    spec = struct((own * tc.shape[0], 2 * block), F32)
    mixed = (spec.shape[0] // 2, 2 * block)
    packed_type = struct((ctx, 2, own, block), BF)
    chan_type = struct((chans, block), BF)

    def exchange(a):
        flat = a.reshape(ctx, 2 * own, block)
        return lax.all_to_all(flat, "ctx", split_axis=0, concat_axis=0, tiled=True).reshape(a.shape)

    rows = out_grad[0]
    anywhere = pl.BlockSpec(memory_space=pl.ANY)
    cuts = pl.pallas_call(
        cut_kernel,
        in_specs=[anywhere],
        out_specs=anywhere,
        out_shape=pltpu.HBM((tp, rows.shape[0], chans), BF),
        scratch_shapes=[
            pltpu.VMEM((tp, rows.shape[0], chans), BF),
            pltpu.SemaphoreType.DMA((2, 2 * tp)),
        ],
    )(hbm(rows))
    rows = lax.all_to_all(cuts, "tp", split_axis=0, concat_axis=0, tiled=True)
    rows = rows.reshape(block, chans)

    grid = 2
    params = pltpu.CompilerParams(vmem_limit_bytes=16 * 2**20)
    half_packed, q_near = pl.pallas_call(
        gated_kernel,
        grid=(grid,),
        in_specs=[cut(k, 0, grid), cut(v, 0, grid), cut(q, 0, grid)],
        out_specs=[cut(packed_type, 0, grid, (1, 0)), cut(q, 0, grid)],
        out_shape=[hbm_out(packed_type), vmem_out(q)],
        compiler_params=params,
    )(hbm(k), hbm(v), hbm(q))
    packed = pl.pallas_call(
        grad_kernel,
        grid=(grid,),
        in_specs=[cut(rows, 1, grid), cut(q, 0, grid), anywhere],
        out_specs=cut(packed_type, 0, grid, (1, 1)),
        out_shape=hbm_out(packed_type),
        input_output_aliases={2: 0},
        compiler_params=params,
    )(rows, vmem(q_near), hbm(half_packed))
    got = exchange(packed)

    taps = filter_taps[0].reshape(own, ctx, block)
    (f_spec,) = call(filter_kernel, 2, [(taps, 0)], (fwd, tc, ts, mf), [(spec, 0)], 20, mixed)
    both, lag_spec = call(
        main_kernel, 2, [(got, 2), (f_spec, 0)], (fwd, back, tc, ts, mf, mi),
        [(hbm_out(packed_type), 2), (hbm_out(struct(spec.shape, BF)), 0)], 32, mixed,
    )
    both = exchange(both)

    halves = back.reshape(dp, ctx // dp, -1)
    half_out = (own, ctx // dp, block)
    lag_own, lag_away = call(
        lag_kernel, 2, [(lag_spec, 0)],
        (
            lax.dynamic_index_in_dim(halves, core, keepdims=False),
            lax.dynamic_index_in_dim(halves, lax.rem(core + 1, dp), keepdims=False),
            tc, ts, mi,
        ),
        [(struct(half_out, F32), 0), (struct(half_out, BF), 0)], 28,
    )
    other = lax.ppermute(lag_away, "dp", [(j, (j + 1) % dp) for j in range(dp)])
    grad_scale = 1.0 / math.sqrt(dp * ctx * block)
    (filter_out,) = call(
        functools.partial(add_kernel, scale=grad_scale), 2, [(lag_own, 0), (other, 0)], (),
        [(hbm_out(struct((own, ctx * block // dp), F32)), 0)], 16,
    )

    filter_out, rows = lax.optimization_barrier((filter_out, rows))
    (near,) = call(
        near_kernel, grid, [(rows, 1), (hbm(k), 0), (hbm(v), 0)], (),
        [(vmem_out(struct((3, chans, block), BF)), 1)], 16,
    )
    query_out, key_out, value_out = call(
        out_kernel, grid,
        [(both, 0), (packed, 0), (vmem(near), 1), (skip_gain[0].reshape(ctx, own), 0)],
        (), [(hbm_out(chan_type), 0)] * 3, 16,
    )
    return (query_out[None], key_out[None], value_out[None], filter_out[None])


def solution(mesh):
    assert mesh.shape["dp"] == 2
    in_specs = (
        P("dp", "tp", "ctx"),
        P("dp", "tp", "ctx"),
        P("dp", "tp", "ctx"),
        P("dp", ("ctx", "tp"), None),
        P("tp", "ctx", None),
        P("tp", None),
    )
    out_specs = (
        P("dp", "tp", "ctx"),
        P("dp", "tp", "ctx"),
        P("dp", "tp", "ctx"),
        P("tp", "ctx", "dp"),
    )
    return jax.shard_map(local, mesh=mesh, in_specs=in_specs, out_specs=out_specs, check_vma=False)
```

```python
import functools
import math

import jax
import jax.numpy as jnp
import numpy as np
from jax import lax
from jax.experimental import pallas as pl
from jax.experimental.pallas import tpu as pltpu
from jax.sharding import PartitionSpec as P

BF = jnp.bfloat16
F32 = jnp.float32


def angle(rows, cols, modulus):
    product = np.arange(rows)[:, None] * np.arange(cols)[None, :] % modulus
    return product.astype(np.float32) * np.float32(2.0 * math.pi / modulus)


def make_tables(block_rows, local_len, factor):
    half = block_rows // 2
    kept = half + 1
    rows = -(-kept // 16) * 16
    real = (np.arange(rows) < kept).astype(np.float32)[:, None]
    weight = np.where((np.arange(rows) == 0) | (np.arange(rows) == half), 1.0, 2.0)[:, None] * real
    fwd = angle(rows, half, block_rows)
    fwd_rows = np.concatenate([np.cos(fwd) * real, -np.sin(fwd) * real], axis=0)
    back_rows = np.concatenate([np.cos(fwd) * weight, -np.sin(fwd) * weight], axis=0).T * factor
    twid = angle(rows, local_len, block_rows * local_len)
    small = angle(local_len, local_len, local_len)
    c, s = np.cos(small), -np.sin(small)
    mat_fwd = np.block([[c, s], [-s, c]])
    mat_inv = np.block([[c, -s], [s, c]])
    pair = lambda a: np.concatenate([a, a], axis=1)
    return (
        jnp.asarray(fwd_rows, BF),
        jnp.asarray(back_rows, BF),
        jnp.asarray(pair(np.cos(twid)), F32),
        jnp.asarray(pair(-np.sin(twid)), F32),
        jnp.asarray(mat_fwd, BF),
        jnp.asarray(mat_inv, BF),
    )


def dot(a, b):
    return jnp.dot(a, b, preferred_element_type=F32)


def forward(blocks, fwd, tcos, tsin, mat, mixed):
    rows = fwd.shape[0] // 2
    n = blocks[0].shape[-1]
    tc, ts = tcos[...], tsin[...]
    for c in range(0, len(blocks), 2):
        a = dot(fwd[...], jnp.concatenate(blocks[c : c + 2], axis=-1))
        ar, ai = a[:rows], a[rows:]
        re = (ar * tc - ai * ts).astype(BF)
        im = (ar * ts + ai * tc).astype(BF)
        for j in range(2):
            at = pl.ds((c + j) * rows, rows)
            mixed[at, :n] = re[:, j * n : (j + 1) * n]
            mixed[at, n:] = im[:, j * n : (j + 1) * n]
    return dot(mixed[...], mat[...])


def join(re, im):
    return jnp.concatenate([re, im], axis=-1).astype(BF)


def inverse(joined, back, tcos, tsin, mat):
    rows = back.shape[1] // 2
    n = joined.shape[-1] // 2
    tc, ts = tcos[...], tsin[...]
    e = dot(joined, mat[...])
    out = []
    for c in range(0, e.shape[0], 2 * rows):
        e0, e1 = e[c : c + rows], e[c + rows : c + 2 * rows]
        er = jnp.concatenate([e0[:, :n], e1[:, :n]], axis=-1)
        ei = jnp.concatenate([e0[:, n:], e1[:, n:]], axis=-1)
        g = jnp.concatenate([er * tc + ei * ts, ei * tc - er * ts], axis=0).astype(BF)
        o = dot(back[...], g)
        out += [o[:, :n], o[:, n:]]
    return out


def split(spec):
    n = spec.shape[-1] // 2
    return spec[:, :n], spec[:, n:]


def by_channel(a):
    a = jnp.swapaxes(a.astype(F32), 0, 1).astype(BF)
    return [a[c] for c in range(a.shape[0])]


def by_block(parts):
    return jnp.swapaxes(jnp.stack(parts), 0, 1).astype(BF)


def cut_kernel(rows, out, held, sems):
    parts, count, width = out.shape
    half = count // 2
    ins, outs = [], []
    for i in range(parts):
        for j in range(2):
            at = pl.ds(j * half, half)
            n = 2 * i + j
            here = held.at[i, at]
            ins.append(
                pltpu.make_async_copy(rows.at[at, pl.ds(i * width, width)], here, sems.at[0, n])
            )
            outs.append(pltpu.make_async_copy(here, out.at[i, at], sems.at[1, n]))
    for copy in ins:
        copy.start()
    for copy, back in zip(ins, outs):
        copy.wait()
        back.start()
    for back in outs:
        back.wait()


def gated_kernel(k, v, q, packed, q_near):
    q_near[...] = q[...]
    shape = (packed.shape[0],) + packed.shape[2:]
    packed[:, 0] = (k[...].astype(F32) * v[...].astype(F32)).astype(BF).reshape(shape)


def grad_kernel(rows, q, half_packed, packed):
    shape = (packed.shape[0],) + packed.shape[2:]
    packed[:, 0] = (rows[...].astype(F32).T * q[...].astype(F32)).astype(BF).reshape(shape)


def near_kernel(rows, k, v, near):
    near[0] = rows[...].astype(F32).T.astype(BF)
    near[1] = k[...]
    near[2] = v[...]


def filter_kernel(taps, fwd, tc, ts, mf, f_spec, mixed):
    f_spec[...] = forward([taps[c] for c in range(taps.shape[0])], fwd, tc, ts, mf, mixed)


def main_kernel(got, f_spec, *refs):
    tables, both, lag_spec = refs[:6], refs[6], refs[7]
    near, got_v, f_v, both_v, lag_v, mixed, table_sems, sems = (
        refs[8:14], *refs[14:21]
    )
    half = got_v.shape[3]
    rows = f_v.shape[1]
    copy = pltpu.make_async_copy

    def piece(ref, h, p):
        return ref.at[:, p, pl.ds(h * half, half)]

    def span(ref, h):
        return ref.at[pl.ds(h * rows, rows)]

    table_in = [copy(t, n, table_sems.at[i]) for i, (t, n) in enumerate(zip(tables, near))]
    got_in = [[copy(piece(got, h, p), got_v.at[h, p], sems.at[0, h, p]) for p in (0, 1)] for h in (0, 1)]
    f_in = [copy(span(f_spec, h), f_v.at[h], sems.at[1, h, 0]) for h in (0, 1)]
    out = [[copy(both_v.at[h, p], piece(both, h, p), sems.at[2, h, p]) for p in (0, 1)] for h in (0, 1)]
    lag_out = [copy(lag_v.at[h], span(lag_spec, h), sems.at[1, h, 1]) for h in (0, 1)]
    got_in[0][0].start()
    for t in table_in:
        t.start()
    f_in[0].start()
    got_in[0][1].start()
    got_in[1][0].start()
    f_in[1].start()
    got_in[1][1].start()
    for t in table_in:
        t.wait()
    fwd, back, tc, ts, mf, mi = near
    for h in (0, 1):
        got_in[h][0].wait()
        xr, xi = split(forward(by_channel(got_v[h, 0]), fwd, tc, ts, mf, mixed))
        f_in[h].wait()
        fr, fi = split(f_v[h])
        both_v[h, 0] = by_block(inverse(join(fr * xr - fi * xi, fr * xi + fi * xr), back, tc, ts, mi))
        out[h][0].start()
        got_in[h][1].wait()
        gr, gi = split(forward(by_channel(got_v[h, 1]), fwd, tc, ts, mf, mixed))
        lag_v[h] = join(xr * gr + xi * gi, xr * gi - xi * gr)
        lag_out[h].start()
        both_v[h, 1] = by_block(inverse(join(fr * gr + fi * gi, fr * gi - fi * gr), back, tc, ts, mi))
        out[h][1].start()
    for h in (0, 1):
        lag_out[h].wait()
        for p in (0, 1):
            out[h][p].wait()


def add_kernel(own, other, out, *, scale):
    total = jnp.swapaxes((own[...] + other[...].astype(F32)) * scale, 0, 1)
    n = total.shape[-1]
    for m in range(total.shape[0]):
        out[:, m * n : (m + 1) * n] = total[m]


def out_kernel(both, packed, near, skip, query_out, key_out, value_out):
    shape = query_out.shape
    tokens, k, v = (near[i].astype(F32) for i in range(3))
    s = lax.broadcast_in_dim(skip[...], skip.shape + (shape[1],), (0, 1))
    conv, corr = (both[:, i].astype(F32) for i in range(2))
    gated, grad = (packed[:, i].astype(F32) for i in range(2))
    through = (conv + s * gated).reshape(shape)
    query_out[...] = (tokens * through).astype(BF)
    total = (corr + s * grad).reshape(shape)
    key_out[...] = (total * v).astype(BF)
    value_out[...] = (total * k).astype(BF)


def lag_kernel(lag_spec, own_rows, away_rows, tc, ts, mi, own, away):
    rows = own_rows.shape[0]
    both = jnp.concatenate([own_rows[...], away_rows[...]], axis=0)
    parts = inverse(lag_spec[...], both, tc, ts, mi)
    for c, part in enumerate(parts):
        own[c] = part[:rows]
        away[c] = part[rows:].astype(BF)


def hbm(a):
    return pltpu.with_memory_space_constraint(a, pltpu.HBM)


def hbm_out(a):
    return pltpu.HBM(a.shape, a.dtype)


def vmem(a):
    return pltpu.with_memory_space_constraint(a, pltpu.VMEM)


def vmem_out(a):
    return pltpu.VMEM(a.shape, a.dtype)


def cut(a, dim, grid, at=None):
    block = [s // grid if i == dim else s for i, s in enumerate(a.shape)]
    index = [0] * len(block)
    if at:
        block[at[0]], index[at[0]] = 1, at[1]
    return pl.BlockSpec(
        tuple(block), lambda g: tuple(g if i == dim else n for i, n in enumerate(index))
    )


def call(body, grid, ins, tables, outs, vmem, mixed=None):
    return pl.pallas_call(
        body,
        grid=(grid,),
        in_specs=[cut(a, d, grid) for a, d in ins] + [cut(a, None, grid) for a in tables],
        out_specs=[cut(a, d, grid) for a, d in outs],
        out_shape=[a for a, _ in outs],
        scratch_shapes=[] if mixed is None else [pltpu.VMEM(mixed, BF)],
        compiler_params=pltpu.CompilerParams(vmem_limit_bytes=vmem * 2**20),
        cost_estimate=pl.CostEstimate(flops=2**20, bytes_accessed=2**20, transcendentals=0),
    )(*[a for a, _ in ins], *[hbm(a) for a in tables])


def local(query_proj, key_proj, value_proj, out_grad, filter_taps, skip_gain):
    ctx = lax.axis_size("ctx")
    tp = lax.axis_size("tp")
    dp = lax.axis_size("dp")
    q, k, v = query_proj[0], key_proj[0], value_proj[0]
    chans, block = q.shape
    own = chans // ctx
    factor = 1.0 / (2 * ctx * block)
    fwd, back, tc, ts, mf, mi = make_tables(2 * ctx, block, factor)
    core = lax.axis_index("dp")
    struct = jax.ShapeDtypeStruct
    spec = struct((own * tc.shape[0], 2 * block), F32)
    mixed = (spec.shape[0] // 2, 2 * block)
    packed_type = struct((ctx, 2, own, block), BF)
    chan_type = struct((chans, block), BF)

    def exchange(a):
        flat = a.reshape(ctx, 2 * own, block)
        return lax.all_to_all(flat, "ctx", split_axis=0, concat_axis=0, tiled=True).reshape(a.shape)

    rows = out_grad[0]
    anywhere = pl.BlockSpec(memory_space=pl.ANY)
    cuts = pl.pallas_call(
        cut_kernel,
        in_specs=[anywhere],
        out_specs=anywhere,
        out_shape=pltpu.HBM((tp, rows.shape[0], chans), BF),
        scratch_shapes=[
            pltpu.VMEM((tp, rows.shape[0], chans), BF),
            pltpu.SemaphoreType.DMA((2, 2 * tp)),
        ],
    )(hbm(rows))
    rows = lax.all_to_all(cuts, "tp", split_axis=0, concat_axis=0, tiled=True)
    rows = rows.reshape(block, chans)

    grid = 2
    params = pltpu.CompilerParams(vmem_limit_bytes=16 * 2**20)
    half_packed, q_near = pl.pallas_call(
        gated_kernel,
        grid=(grid,),
        in_specs=[cut(k, 0, grid), cut(v, 0, grid), cut(q, 0, grid)],
        out_specs=[cut(packed_type, 0, grid, (1, 0)), cut(q, 0, grid)],
        out_shape=[hbm_out(packed_type), vmem_out(q)],
        compiler_params=params,
    )(hbm(k), hbm(v), hbm(q))
    packed = pl.pallas_call(
        grad_kernel,
        grid=(grid,),
        in_specs=[cut(rows, 1, grid), cut(q, 0, grid), anywhere],
        out_specs=cut(packed_type, 0, grid, (1, 1)),
        out_shape=hbm_out(packed_type),
        input_output_aliases={2: 0},
        compiler_params=params,
    )(rows, vmem(q_near), hbm(half_packed))
    got = exchange(packed)

    taps = filter_taps[0].reshape(own, ctx, block)
    (f_spec,) = call(filter_kernel, 2, [(taps, 0)], (fwd, tc, ts, mf), [(spec, 0)], 20, mixed)
    tables = (fwd, back, tc, ts, mf, mi)
    both, lag_spec = pl.pallas_call(
        main_kernel,
        in_specs=[anywhere] * 8,
        out_specs=[anywhere] * 2,
        out_shape=[hbm_out(packed_type), pltpu.HBM(spec.shape, BF)],
        scratch_shapes=[pltpu.VMEM(t.shape, t.dtype) for t in tables]
        + [
            pltpu.VMEM((2, 2, ctx, own // 2, block), BF),
            pltpu.VMEM((2, spec.shape[0] // 2, spec.shape[1]), F32),
            pltpu.VMEM((2, 2, ctx, own // 2, block), BF),
            pltpu.VMEM((2, spec.shape[0] // 2, spec.shape[1]), BF),
            pltpu.VMEM(mixed, BF),
            pltpu.SemaphoreType.DMA((len(tables),)),
            pltpu.SemaphoreType.DMA((3, 2, 2)),
        ],
        compiler_params=pltpu.CompilerParams(vmem_limit_bytes=32 * 2**20),
        cost_estimate=pl.CostEstimate(flops=2**20, bytes_accessed=2**20, transcendentals=0),
    )(got, f_spec, *[hbm(t) for t in tables])
    both = exchange(both)

    halves = back.reshape(dp, ctx // dp, -1)
    half_out = (own, ctx // dp, block)
    lag_own, lag_away = call(
        lag_kernel, 2, [(lag_spec, 0)],
        (
            lax.dynamic_index_in_dim(halves, core, keepdims=False),
            lax.dynamic_index_in_dim(halves, lax.rem(core + 1, dp), keepdims=False),
            tc, ts, mi,
        ),
        [(struct(half_out, F32), 0), (struct(half_out, BF), 0)], 28,
    )
    other = lax.ppermute(lag_away, "dp", [(j, (j + 1) % dp) for j in range(dp)])
    grad_scale = 1.0 / math.sqrt(dp * ctx * block)
    (filter_out,) = call(
        functools.partial(add_kernel, scale=grad_scale), 2, [(lag_own, 0), (other, 0)], (),
        [(hbm_out(struct((own, ctx * block // dp), F32)), 0)], 16,
    )

    filter_out, rows = lax.optimization_barrier((filter_out, rows))
    (near,) = call(
        near_kernel, grid, [(rows, 1), (hbm(k), 0), (hbm(v), 0)], (),
        [(vmem_out(struct((3, chans, block), BF)), 1)], 16,
    )
    query_out, key_out, value_out = call(
        out_kernel, grid,
        [(both, 0), (packed, 0), (vmem(near), 1), (skip_gain[0].reshape(ctx, own), 0)],
        (), [(hbm_out(chan_type), 0)] * 3, 16,
    )
    return (query_out[None], key_out[None], value_out[None], filter_out[None])


def solution(mesh):
    assert mesh.shape["dp"] == 2
    in_specs = (
        P("dp", "tp", "ctx"),
        P("dp", "tp", "ctx"),
        P("dp", "tp", "ctx"),
        P("dp", ("ctx", "tp"), None),
        P("tp", "ctx", None),
        P("tp", None),
    )
    out_specs = (
        P("dp", "tp", "ctx"),
        P("dp", "tp", "ctx"),
        P("dp", "tp", "ctx"),
        P("tp", "ctx", "dp"),
    )
    return jax.shard_map(local, mesh=mesh, in_specs=in_specs, out_specs=out_specs, check_vma=False)
```
